32 devices in a mesh: row: 8 (over y, x, core), col: 4 (over z).
Axes of the slice: x: 2, y: 2, z: 4, core: 2. Of those that a mesh axis runs over, the one named last changes fastest.
Arguments:
- left_rows: float32 [256, 61440], P('col', 'row'), may hold values from -1.2 to 1.2
- right_cols: float32 [61440, 2048], P('col', 'row'), may hold values from -1.2 to 1.2
- left_pattern: int32 [4, 240], replicated, may hold values from 0 to 1, as said below
- right_pattern: int32 [240, 8], replicated, may hold values from 0 to 1, as said below
Outputs:
- square_terms: float32 [256, 2048], P('col', 'row')
The draws below stay inside these ranges and needn't reach their ends.
Inputs may be any that keep to these rules, and one draw needn't show every extreme that they name: Every device's tile of left_pattern (row b, inner blocks from a * 30) has between 1 and 7 occupied blocks, and some tile has exactly 7 in every draw. Every device's tile of right_pattern (inner blocks from b * 60, column a) has between 1 and 15 occupied blocks, and some tile has exactly 15 in every draw.
All inputs are finite; a program needn't handle non-finite values.
Results may differ from the reference program's by a relative error of at most 0.0001.
Values sent between devices are 32-bit elements; how exact they have to be, the bound alone decides.
A program may use at most 192 MiB of HBM per device.

```python
import jax
import jax.numpy as jnp
from jax import lax

BLK = 256
NBLK = 240
LROWS = 64
STEPS = 4
BPD = 30
TROWS = 60
LCAP = 7
RCAP = 15
ORDER = 61440
WROWS = 256
WCOLS = 2048
N_ROW = 8
N_COL = 4


def occupied_tiles(key, tile_count, tile_blocks, most):
    extra_key = jax.random.fold_in(key, 1)
    busy_key = jax.random.fold_in(key, 2)
    pick_key = jax.random.fold_in(key, 3)
    order_key = jax.random.fold_in(key, 4)
    extra = jax.random.randint(extra_key, (tile_count,), 2, most + 1)
    busy = jax.random.randint(busy_key, (tile_count,), 0, 4) == 0
    counts = jnp.where(busy, extra, 1)
    chosen = jax.random.randint(pick_key, (), 0, tile_count)
    counts = jnp.where(jnp.arange(tile_count) == chosen, most, counts)
    permuted = jax.vmap(lambda subkey: jax.random.permutation(subkey, tile_blocks))(jax.random.split(order_key, tile_count))
    ranked = jnp.argsort(permuted, axis=1)
    return (ranked < counts[:, None]).astype(jnp.int32)


def draw_left_pattern(key, part):
    occupied = occupied_tiles(jax.random.fold_in(key, 17), N_COL * N_ROW, BPD, LCAP)
    return occupied.reshape(N_COL, N_ROW * BPD)


def draw_right_pattern(key, part):
    occupied = occupied_tiles(jax.random.fold_in(key, 29), N_COL * N_ROW, TROWS, RCAP)
    return occupied.reshape(N_COL, N_ROW, TROWS).transpose(0, 2, 1).reshape(N_COL * TROWS, N_ROW)


def levels(rng, dims, pieces, least, high):
    def one(axis_at, parts):
        draws = jax.random.uniform(jax.random.fold_in(jax.random.fold_in(rng, 6), axis_at), (parts,), jnp.float32, least / len(pieces), high / len(pieces))
        return jnp.repeat(jnp.exp(draws), dims[axis_at] // parts).reshape((-1,) + (1,) * (len(dims) - axis_at - 1))

    factor_of = one(*pieces[0])
    for cut in pieces[1:]:
        factor_of = factor_of * one(*cut)
    return factor_of


def normal_values(own_key, shape, deviation, reach, cuts=(), held_as=jnp.bfloat16):
    result = deviation * jax.random.normal(own_key, shape, jnp.float32)
    if cuts:
        result = result * levels(own_key, shape, cuts, -0.22, 0.18)
    return jnp.clip(result, -reach, reach).astype(held_as)


def setup_inputs(seed: int = 0) -> dict:
    seeds = jax.random.split(jax.random.key(seed), 5)
    return {
        "left_rows": normal_values(seeds[0], (WROWS, ORDER), 0.2, 1.2, ((0, 4), (1, 8)), jnp.float32),
        "right_cols": normal_values(seeds[1], (ORDER, WCOLS), 0.2, 1.2, ((0, 4), (1, 8)), jnp.float32),
        "left_pattern": draw_left_pattern(jax.random.fold_in(seeds[4], 71), 0),
        "right_pattern": draw_right_pattern(jax.random.fold_in(seeds[4], 71), 0),
    }


def reference(left_rows, right_cols, left_pattern, right_pattern):
    left_mask = left_pattern.astype(jnp.float32)
    right_mask = right_pattern.astype(jnp.float32)
    left_masked = (left_rows.reshape(N_COL, LROWS, NBLK, BLK) * left_mask[:, None, :, None]).reshape(N_COL * LROWS, NBLK * BLK)
    right_masked = (right_cols.reshape(NBLK, BLK, N_ROW, BLK) * right_mask[:, None, :, None]).reshape(NBLK * BLK, N_ROW * BLK)
    ratio = N_ROW // N_COL
    inner = BPD * BLK
    panels = []
    for column in range(N_COL):
        total = jnp.zeros((LROWS, N_ROW * BLK), jnp.float32)
        for step in range(STEPS):
            inner_panel = (column * ratio + step) % N_ROW
            left = left_masked[column * LROWS:(column + 1) * LROWS, inner_panel * inner:(inner_panel + 1) * inner]
            right = right_masked[inner_panel * inner:(inner_panel + 1) * inner, :]
            total = total + jnp.dot(left, right, precision=lax.Precision.HIGHEST, preferred_element_type=jnp.float32)
        panels.append(total)
    return jnp.concatenate(panels, axis=0)
```

```python
import functools

import jax
import jax.numpy as jnp
from jax import lax
from jax.experimental import pallas as pl
from jax.experimental.pallas import tpu as pltpu
from jax.sharding import PartitionSpec as P

STEPS = 4
STRIP = 8
MESH = pl.DeviceIdType.MESH


def prepare(dims, lpat, rpat, left, tab_idx, tab_mask, packed, own_idx, sems):
    nrow, ncol, ratio, per_k, cap, blk = dims
    r = lax.axis_index("row")
    c = lax.axis_index("col")
    for i in range(cap):
        own_idx[i] = 0

    def own_step(u, count):
        flag = lpat[c, r * per_k + u]

        @pl.when(flag != 0)
        def _():
            own_idx[count] = u

        return count + flag

    lax.fori_loop(0, per_k, own_step, 0)
    copies = []
    for i in range(cap):
        at = pl.multiple_of(own_idx[i] * blk, blk)
        copy = pltpu.make_async_copy(left.at[:, pl.ds(at, blk)], packed.at[i], sems.at[i])
        copy.start()
        copies.append(copy)
    for i in range(STEPS * cap):
        tab_idx[i] = 0
        tab_mask[i] = jnp.float32(0)
    for t in range(STEPS):
        d, j = divmod(t, ratio)
        b = lax.rem(c - d + ncol, ncol)
        base = (c * ratio + j) * per_k

        def step(u, count):
            flag = lpat[b, base + u]

            @pl.when(flag != 0)
            def _():
                tab_idx[t * cap + count] = j * per_k + u
                tab_mask[t * cap + count] = (rpat[base + u, r] != 0).astype(jnp.float32)

            return count + flag

        lax.fori_loop(0, per_k, step, 0)
    for copy in copies:
        copy.wait()


def split(x):
    high = x.astype(jnp.bfloat16)
    low = (x - high.astype(jnp.float32)).astype(jnp.bfloat16)
    return high, low


def dot(a, b):
    return jnp.dot(a, b, preferred_element_type=jnp.float32)


def exchange(dims, tab_idx, tab_mask, packed, right, out, held, right_v, total, came, right_sem, send1, recv1,
             send2, recv2, send3, recv3):
    nrow, ncol, ratio, per_k, cap, blk = dims
    shifts = STEPS // ratio
    strips = packed.shape[1] // STRIP
    parts = nrow // strips
    width = blk // parts
    r = lax.axis_index("row")
    c = lax.axis_index("col")
    load = pltpu.make_async_copy(right, right_v, right_sem)
    load.start()

    barrier = pltpu.get_barrier_semaphore()
    for s in range(1, nrow):
        pl.semaphore_signal(barrier, inc=1, device_id=(lax.rem(r + s, nrow), c), device_id_type=MESH)
    for d in range(1, shifts):
        behind = lax.rem(c - d + ncol, ncol)
        ahead = lax.rem(c + d, ncol)
        for j in range(ratio):
            pl.semaphore_signal(barrier, inc=1, device_id=(c * ratio + j, behind), device_id_type=MESH)
        pl.semaphore_signal(barrier, inc=1, device_id=(r, ahead), device_id_type=MESH)
    goal = r // ratio
    my_d = lax.rem(goal - c + ncol, ncol)
    my_j = lax.rem(r, ratio)
    base = nrow - 1 + shifts - 1
    sends = jnp.logical_and(my_d >= 1, my_d < shifts)
    pl.semaphore_wait(barrier, jnp.where(sends, base + nrow, base))

    def piece(p):
        row = lax.rem(p, strips)
        part = p // strips
        rows = pl.ds(pl.multiple_of(row * STRIP, STRIP), STRIP)
        if parts == 1:
            return packed.at[:, rows, :]
        return packed.at[:, rows, pl.ds(pl.multiple_of(part * width, width), width)]

    def scatter(d, s):
        t = d * ratio + my_j
        p = lax.rem(r + s, nrow)
        return pltpu.make_async_remote_copy(
            src_ref=piece(p), dst_ref=held.at[t, p], send_sem=send1.at[s], recv_sem=recv1.at[t],
            device_id=(p, lax.rem(c + d, ncol)), device_id_type=MESH)

    def keep():
        return pltpu.make_async_copy(piece(r), held.at[my_j, r], recv1.at[my_j])

    for d in range(shifts):
        @pl.when(my_d == d)
        def _():
            if d == 0:
                keep().start()
            for s in range(1 if d == 0 else 0, nrow):
                scatter(d, s).start()

    def spread(t, s):
        return pltpu.make_async_remote_copy(
            src_ref=held.at[t, r], dst_ref=held.at[t, r], send_sem=send2.at[t, s], recv_sem=recv2.at[t, s],
            device_id=(lax.rem(r + s, nrow), c), device_id_type=MESH)

    def arrived(t, s):
        p = lax.rem(r - s + nrow, nrow)
        return pltpu.make_async_remote_copy(
            src_ref=held.at[t, p], dst_ref=held.at[t, p], send_sem=send2.at[t, s], recv_sem=recv2.at[t, s],
            device_id=(p, c), device_id_type=MESH)

    for t in range(STEPS):
        pltpu.make_async_copy(held.at[t, r], held.at[t, r], recv1.at[t]).wait()
        for s in range(1, nrow):
            spread(t, s).start()
    load.wait()
    total[...] = jnp.zeros_like(total)

    def give(d):
        return pltpu.make_async_remote_copy(
            src_ref=total.at[d], dst_ref=came.at[d], send_sem=send3.at[d], recv_sem=recv3.at[d],
            device_id=(r, lax.rem(c - d + ncol, ncol)), device_id_type=MESH)

    for d in range(shifts):
        for j in range(ratio):
            t = d * ratio + j
            for s in range(1, nrow):
                arrived(t, s).wait_recv()

            def term(i, acc):
                at = t * cap + i
                pieces = [
                    held[t, pl.ds(part * strips, strips), i].reshape(strips * STRIP, width) for part in range(parts)
                ]
                block = (pieces[0] if parts == 1 else jnp.concatenate(pieces, axis=1)) * tab_mask[at]
                other = right_v[tab_idx[at]]
                a_high, a_low = split(block)
                b_high, b_low = split(other)
                return acc + (dot(a_high, b_high) + (dot(a_high, b_low) + dot(a_low, b_high)))

            total[d] = lax.fori_loop(0, cap, term, total[d])
        if d > 0:
            give(d).start()

    result = total[0]
    for d in range(1, shifts):
        give(d).wait_recv()
        result = result + came[d]
    out[...] = result
    for d in range(1, shifts):
        give(d).wait_send()
    for d in range(shifts):
        @pl.when(my_d == d)
        def _():
            for s in range(1 if d == 0 else 0, nrow):
                scatter(d, s).wait_send()
    for t in range(STEPS):
        for s in range(1, nrow):
            spread(t, s).wait_send()


def body(left_rows, right_cols, left_pattern, right_pattern):
    nrow = lax.axis_size("row")
    ncol = lax.axis_size("col")
    ratio = nrow // ncol
    lrows, left_width = left_rows.shape
    right_height, blk = right_cols.shape
    per_k = left_width // blk
    trows = right_height // blk
    cap = per_k // 4
    shifts = STEPS // ratio
    strips = lrows // STRIP
    dims = (nrow, ncol, ratio, per_k, cap, blk)
    smem = pl.BlockSpec(memory_space=pltpu.SMEM)
    vmem = pl.BlockSpec(memory_space=pltpu.VMEM)
    anywhere = pl.BlockSpec(memory_space=pl.ANY)
    tab_idx, tab_mask, packed = pl.pallas_call(
        functools.partial(prepare, dims),
        out_shape=(
            jax.ShapeDtypeStruct((STEPS * cap,), jnp.int32),
            jax.ShapeDtypeStruct((STEPS * cap,), jnp.float32),
            jax.ShapeDtypeStruct((cap, lrows, blk), jnp.float32),
        ),
        in_specs=[smem, smem, anywhere],
        out_specs=(smem, smem, vmem),
        scratch_shapes=[pltpu.SMEM((cap,), jnp.int32), pltpu.SemaphoreType.DMA((cap,))],
        name="prepare",
    )(left_pattern, right_pattern, left_rows)
    parts = nrow // strips
    dma = pltpu.SemaphoreType.DMA
    return pl.pallas_call(
        functools.partial(exchange, dims),
        out_shape=jax.ShapeDtypeStruct((lrows, blk), jnp.float32),
        in_specs=[smem, smem, vmem, anywhere],
        out_specs=vmem,
        scratch_shapes=[
            pltpu.VMEM((STEPS, nrow, cap, STRIP, blk // parts), jnp.float32),
            pltpu.VMEM((trows, blk, blk), jnp.float32),
            pltpu.VMEM((shifts, lrows, blk), jnp.float32),
            pltpu.VMEM((shifts, lrows, blk), jnp.float32),
            dma, dma((nrow,)), dma((STEPS,)), dma((STEPS, nrow)), dma((STEPS, nrow)), dma((shifts,)), dma((shifts,)),
        ],
        compiler_params=pltpu.CompilerParams(
            collective_id=0, has_side_effects=True, vmem_limit_bytes=40 * 1024 * 1024),
        name="exchange",
    )(tab_idx, tab_mask, packed, right_cols.reshape(trows, blk, blk))


def solution(mesh):
    return jax.shard_map(
        body,
        mesh=mesh,
        in_specs=(P("col", "row"), P("col", "row"), P(), P()),
        out_specs=P("col", "row"),
        check_vma=False,
    )
```

```python
import functools

import jax
import jax.numpy as jnp
from jax import lax
from jax.experimental import pallas as pl
from jax.experimental.pallas import tpu as pltpu
from jax.sharding import PartitionSpec as P

STEPS = 4
STRIP = 8
SIZES = (2, 4)
MESH = pl.DeviceIdType.MESH


def choose(dims, sizes, lpat, rpat, need, pick):
    nrow, ncol, ratio, per_k, cap, blk = dims
    shifts = STEPS // ratio
    useful = (lpat[...] != 0) & (jnp.max(rpat[...], axis=0, keepdims=True) != 0)
    useful = useful.astype(jnp.int32)
    need[...] = useful
    at = lax.broadcasted_iota(jnp.int32, useful.shape, 1)
    b = lax.broadcasted_iota(jnp.int32, (ncol, 1), 0)
    most = jnp.zeros((ncol, 1), jnp.int32)
    for q in range(nrow):
        inside = (at >= q * per_k) & (at < (q + 1) * per_k)
        count = jnp.sum(jnp.where(inside, useful, 0), axis=1, keepdims=True)
        d = lax.rem(q // ratio - b + ncol, ncol)
        most = jnp.maximum(most, jnp.where(d < shifts, count, 0))
    top = jnp.max(most)
    index = jnp.int32(0)
    for size in sizes[:-1]:
        index = index + (top > size).astype(jnp.int32)
    pick[0] = index


def split(x):
    high = x.astype(jnp.bfloat16)
    low = (x - high.astype(jnp.float32)).astype(jnp.bfloat16)
    return high, low


def dot(a, b):
    return jnp.dot(a, b, preferred_element_type=jnp.float32)


def listed(need, row, base, per_k, cap):
    def step(u, state):
        count, slots = state[0], state[1:]
        flag = need[row, base + u]
        slots = [slot + u * flag * (count == i).astype(jnp.int32) for i, slot in enumerate(slots)]
        return (count + flag, *slots)

    return lax.fori_loop(0, per_k, step, (jnp.int32(0),) * (cap + 1))


def exchange(dims, need, rpat, left, right, out, left_v, packed, held, right_v, total, came, tab_idx, tab_mask,
             left_sem, right_sem, send1, recv1, send2, recv2, send3, recv3):
    nrow, ncol, ratio, per_k, cap, blk = dims
    shifts = STEPS // ratio
    strips = left.shape[0] // STRIP
    parts = nrow // strips
    width = blk // parts
    r = lax.axis_index("row")
    c = lax.axis_index("col")
    goal = r // ratio
    my_d = lax.rem(goal - c + ncol, ncol)
    my_j = lax.rem(r, ratio)

    @pl.when(my_d < shifts)
    def _():
        for u in range(per_k):
            pltpu.make_async_copy(left.at[:, pl.ds(u * blk, blk)], left_v.at[u], left_sem).start()

    load = pltpu.make_async_copy(right, right_v, right_sem)

    barrier = pltpu.get_barrier_semaphore()
    for s in range(1, nrow):
        pl.semaphore_signal(barrier, inc=1, device_id=(lax.rem(r + s, nrow), c), device_id_type=MESH)
    for d in range(1, shifts):
        behind = lax.rem(c - d + ncol, ncol)
        ahead = lax.rem(c + d, ncol)
        for j in range(ratio):
            pl.semaphore_signal(barrier, inc=1, device_id=(c * ratio + j, behind), device_id_type=MESH)
        pl.semaphore_signal(barrier, inc=1, device_id=(r, ahead), device_id_type=MESH)

    @pl.when(my_d < shifts)
    def _():
        found = listed(need, c, r * per_k, per_k, cap)
        pltpu.make_async_copy(left_v, left_v, left_sem).wait()
        for i in range(cap):
            block = left_v[found[1 + i]]
            for p in range(nrow):
                row, part = p % strips, p // strips
                packed[p, i] = block[row * STRIP:(row + 1) * STRIP, part * width:(part + 1) * width]

    base = nrow - 1 + shifts - 1
    sends = jnp.logical_and(my_d >= 1, my_d < shifts)
    pl.semaphore_wait(barrier, jnp.where(sends, base + nrow, base))

    def scatter(d, s):
        t = d * ratio + my_j
        p = lax.rem(r + s, nrow)
        return pltpu.make_async_remote_copy(
            src_ref=packed.at[p], dst_ref=held.at[t, p], send_sem=send1.at[s], recv_sem=recv1.at[t],
            device_id=(p, lax.rem(c + d, ncol)), device_id_type=MESH)

    def keep():
        return pltpu.make_async_copy(packed.at[r], held.at[my_j, r], recv1.at[my_j])

    for d in range(shifts):
        @pl.when(my_d == d)
        def _():
            if d == 0:
                keep().start()
            for s in range(1 if d == 0 else 0, nrow):
                scatter(d, s).start()

    def spread(t, s):
        return pltpu.make_async_remote_copy(
            src_ref=held.at[t, r], dst_ref=held.at[t, r], send_sem=send2.at[t, s], recv_sem=recv2.at[t, s],
            device_id=(lax.rem(r + s, nrow), c), device_id_type=MESH)

    def arrived(t, s):
        p = lax.rem(r - s + nrow, nrow)
        return pltpu.make_async_remote_copy(
            src_ref=held.at[t, p], dst_ref=held.at[t, p], send_sem=send2.at[t, s], recv_sem=recv2.at[t, s],
            device_id=(p, c), device_id_type=MESH)

    load.start()
    for t in range(STEPS):
        d, j = divmod(t, ratio)
        found = listed(need, lax.rem(c - d + ncol, ncol), (c * ratio + j) * per_k, per_k, cap)
        for i in range(cap):
            u = found[1 + i]
            tab_idx[t * cap + i] = j * per_k + u
            both = (found[0] > i).astype(jnp.int32) * rpat[r, (c * ratio + j) * per_k + u]
            tab_mask[t * cap + i] = both.astype(jnp.float32)
    total[...] = jnp.zeros_like(total)

    for t in range(STEPS):
        pltpu.make_async_copy(held.at[t, r], held.at[t, r], recv1.at[t]).wait()
        for s in range(1, nrow):
            spread(t, s).start()
    load.wait()

    def give(d):
        return pltpu.make_async_remote_copy(
            src_ref=total.at[d], dst_ref=came.at[d], send_sem=send3.at[d], recv_sem=recv3.at[d],
            device_id=(r, lax.rem(c - d + ncol, ncol)), device_id_type=MESH)

    for d in range(shifts):
        for j in range(ratio):
            t = d * ratio + j
            for s in range(1, nrow):
                arrived(t, s).wait_recv()

            def term(i, acc):
                at = t * cap + i
                pieces = [
                    held[t, pl.ds(part * strips, strips), i].reshape(strips * STRIP, width) for part in range(parts)
                ]
                block = (pieces[0] if parts == 1 else jnp.concatenate(pieces, axis=1)) * tab_mask[at]
                other = right_v[tab_idx[at]]
                a_high, a_low = split(block)
                b_high, b_low = split(other)
                return acc + (dot(a_high, b_high) + (dot(a_high, b_low) + dot(a_low, b_high)))

            total[d] = lax.fori_loop(0, cap, term, total[d])
        if d > 0:
            give(d).start()

    result = total[0]
    for d in range(1, shifts):
        give(d).wait_recv()
        result = result + came[d]
    out[...] = result
    for d in range(1, shifts):
        give(d).wait_send()
    for d in range(shifts):
        @pl.when(my_d == d)
        def _():
            for s in range(1 if d == 0 else 0, nrow):
                scatter(d, s).wait_send()
    for t in range(STEPS):
        for s in range(1, nrow):
            spread(t, s).wait_send()


def body(left_rows, right_cols, left_pattern, right_pattern):
    nrow = lax.axis_size("row")
    ncol = lax.axis_size("col")
    ratio = nrow // ncol
    lrows, left_width = left_rows.shape
    right_height, blk = right_cols.shape
    per_k = left_width // blk
    trows = right_height // blk
    cap = per_k // 4
    shifts = STEPS // ratio
    strips = lrows // STRIP
    sizes = [size for size in SIZES if size < cap] + [cap]
    smem = pl.BlockSpec(memory_space=pltpu.SMEM)
    vmem = pl.BlockSpec(memory_space=pltpu.VMEM)
    anywhere = pl.BlockSpec(memory_space=pl.ANY)
    across = right_pattern.T
    need, pick = pl.pallas_call(
        functools.partial(choose, (nrow, ncol, ratio, per_k, cap, blk), sizes),
        out_shape=(
            jax.ShapeDtypeStruct(left_pattern.shape, jnp.int32),
            jax.ShapeDtypeStruct((1,), jnp.int32),
        ),
        in_specs=[vmem, vmem],
        out_specs=(vmem, smem),
        name="choose",
    )(left_pattern, across)
    parts = nrow // strips
    dma = pltpu.SemaphoreType.DMA

    def run(number, slots):
        return pl.pallas_call(
            functools.partial(exchange, (nrow, ncol, ratio, per_k, slots, blk)),
            out_shape=jax.ShapeDtypeStruct((lrows, blk), jnp.float32),
            in_specs=[smem, smem, anywhere, anywhere],
            out_specs=vmem,
            scratch_shapes=[
                pltpu.VMEM((per_k, lrows, blk), jnp.float32),
                pltpu.VMEM((nrow, slots, STRIP, blk // parts), jnp.float32),
                pltpu.VMEM((STEPS, nrow, slots, STRIP, blk // parts), jnp.float32),
                pltpu.VMEM((trows, blk, blk), jnp.float32),
                pltpu.VMEM((shifts, lrows, blk), jnp.float32),
                pltpu.VMEM((shifts, lrows, blk), jnp.float32),
                pltpu.SMEM((STEPS * slots,), jnp.int32),
                pltpu.SMEM((STEPS * slots,), jnp.float32),
                dma, dma, dma((nrow,)), dma((STEPS,)), dma((STEPS, nrow)), dma((STEPS, nrow)), dma((shifts,)),
                dma((shifts,)),
            ],
            compiler_params=pltpu.CompilerParams(
                collective_id=number, has_side_effects=True, vmem_limit_bytes=60 * 1024 * 1024),
            name="exchange%d" % slots,
        )

    branches = [run(number, slots) for number, slots in enumerate(sizes)]
    inputs = (need, across, left_rows, right_cols.reshape(trows, blk, blk))
    if len(branches) == 1:
        return branches[0](*inputs)
    return lax.switch(pick[0], branches, *inputs)


def solution(mesh):
    return jax.shard_map(
        body,
        mesh=mesh,
        in_specs=(P("col", "row"), P("col", "row"), P(), P()),
        out_specs=P("col", "row"),
        check_vma=False,
    )
```

```python
import functools

import jax
import jax.numpy as jnp
from jax import lax
from jax.experimental import pallas as pl
from jax.experimental.pallas import tpu as pltpu
from jax.sharding import PartitionSpec as P

STEPS = 4
STRIP = 8
SIZES = ((1, 4), (2, 5), (3, 6), (4, 6), (3, 9), (4, 9), (6, 12))
MESH = pl.DeviceIdType.MESH


def choose(dims, sizes, lpat, rpat, need, pick):
    nrow, ncol, ratio, per_k, cap, blk = dims
    shifts = STEPS // ratio
    useful = (lpat[...] != 0) & (jnp.max(rpat[...], axis=0, keepdims=True) != 0)
    useful = useful.astype(jnp.int32)
    need[...] = useful
    at = lax.broadcasted_iota(jnp.int32, useful.shape, 1)
    b = lax.broadcasted_iota(jnp.int32, (ncol, 1), 0)
    most = jnp.zeros((ncol, 1), jnp.int32)
    largest = jnp.zeros((1, 1), jnp.int32)
    for q in range(nrow):
        inside = (at >= q * per_k) & (at < (q + 1) * per_k)
        count = jnp.sum(jnp.where(inside, useful, 0), axis=1, keepdims=True)
        d = lax.rem(q // ratio - b + ncol, ncol)
        count = jnp.where(d < shifts, count, 0)
        most = jnp.maximum(most, count)
        group = count if q % ratio == 0 else group + count
        if q % ratio == ratio - 1:
            largest = jnp.maximum(largest, jnp.sum(group, axis=0, keepdims=True))
    top = jnp.max(most)
    full = jnp.max(largest)
    index = jnp.int32(len(sizes) - 1)
    for k in reversed(range(len(sizes) - 1)):
        index = jnp.where((top <= sizes[k][0]) & (full <= sizes[k][1]), k, index)
    pick[0] = index


def split(x):
    high = x.astype(jnp.bfloat16)
    low = (x - high.astype(jnp.float32)).astype(jnp.bfloat16)
    return high, low


def dot(a, b):
    return jnp.dot(a, b, preferred_element_type=jnp.float32)


def listed(need, row, base, per_k, state, shift=0):
    def step(u, state):
        count, slots = state[0], state[1:]
        flag = need[row, base + u]
        slots = [slot + (u + shift) * flag * (count == i).astype(jnp.int32) for i, slot in enumerate(slots)]
        return (count + flag, *slots)

    return lax.fori_loop(0, per_k, step, state)


def exchange(dims, need, rpat, left, right, out, left_v, packed, landed, held, right_v, total, came, tab_idx,
             tab_mask, left_sem, right_sem, send1, recv1, send2, recv2, send3, recv3):
    nrow, ncol, ratio, per_k, cap, room, blk = dims
    shifts = STEPS // ratio
    strips = left.shape[0] // STRIP
    parts = nrow // strips
    width = blk // parts
    r = lax.axis_index("row")
    c = lax.axis_index("col")
    goal = r // ratio
    my_d = lax.rem(goal - c + ncol, ncol)
    my_j = lax.rem(r, ratio)

    @pl.when(my_d < shifts)
    def _():
        for u in range(per_k):
            pltpu.make_async_copy(left.at[:, pl.ds(u * blk, blk)], left_v.at[u], left_sem).start()

    load = pltpu.make_async_copy(right, right_v, right_sem)

    barrier = pltpu.get_barrier_semaphore()
    for s in range(1, nrow):
        pl.semaphore_signal(barrier, inc=1, device_id=(lax.rem(r + s, nrow), c), device_id_type=MESH)
    for d in range(1, shifts):
        behind = lax.rem(c - d + ncol, ncol)
        ahead = lax.rem(c + d, ncol)
        for j in range(ratio):
            pl.semaphore_signal(barrier, inc=1, device_id=(c * ratio + j, behind), device_id_type=MESH)
        pl.semaphore_signal(barrier, inc=1, device_id=(r, ahead), device_id_type=MESH)

    @pl.when(my_d < shifts)
    def _():
        found = listed(need, c, r * per_k, per_k, (jnp.int32(0),) * (cap + 1))
        pltpu.make_async_copy(left_v, left_v, left_sem).wait()
        for i in range(cap):
            block = left_v[found[1 + i]]
            for p in range(nrow):
                row, part = p % strips, p // strips
                packed[p, i] = block[row * STRIP:(row + 1) * STRIP, part * width:(part + 1) * width]

    base = nrow - 1 + shifts - 1
    sends = jnp.logical_and(my_d >= 1, my_d < shifts)
    pl.semaphore_wait(barrier, jnp.where(sends, base + nrow, base))

    def scatter(d, s):
        t = d * ratio + my_j
        p = lax.rem(r + s, nrow)
        return pltpu.make_async_remote_copy(
            src_ref=packed.at[p], dst_ref=landed.at[pl.ds(t * cap, cap)], send_sem=send1.at[s], recv_sem=recv1.at[t],
            device_id=(p, lax.rem(c + d, ncol)), device_id_type=MESH)

    def keep():
        return pltpu.make_async_copy(packed.at[r], landed.at[pl.ds(my_j * cap, cap)], recv1.at[my_j])

    for d in range(shifts):
        @pl.when(my_d == d)
        def _():
            if d == 0:
                keep().start()
            for s in range(1 if d == 0 else 0, nrow):
                scatter(d, s).start()

    def spread(s):
        return pltpu.make_async_remote_copy(
            src_ref=held.at[r], dst_ref=held.at[r], send_sem=send2.at[s], recv_sem=recv2.at[s],
            device_id=(lax.rem(r + s, nrow), c), device_id_type=MESH)

    def arrived(s):
        p = lax.rem(r - s + nrow, nrow)
        return pltpu.make_async_remote_copy(
            src_ref=held.at[p], dst_ref=held.at[p], send_sem=send2.at[s], recv_sem=recv2.at[s],
            device_id=(p, c), device_id_type=MESH)

    load.start()
    state = (jnp.int32(0),) * (room + 1)
    starts = [jnp.int32(0)]
    for t in range(STEPS):
        d, j = divmod(t, ratio)
        state = listed(need, lax.rem(c - d + ncol, ncol), (c * ratio + j) * per_k, per_k, state, j * per_k)
        starts.append(state[0])
    sources = []
    for g in range(room):
        source = jnp.int32(0)
        both = rpat[r, c * ratio * per_k + state[1 + g]]
        tab_idx[g] = state[1 + g]
        weights = [jnp.int32(0)] * shifts
        for t in range(STEPS):
            inside = (starts[t] <= g).astype(jnp.int32) * (starts[t + 1] > g).astype(jnp.int32)
            source = source + inside * (t * cap + g - starts[t])
            weights[t // ratio] = weights[t // ratio] + inside
        for d in range(shifts):
            tab_mask[d * room + g] = (weights[d] * both).astype(jnp.float32)
        sources.append(source)
    for t in range(STEPS):
        part = landed.at[pl.ds(t * cap, cap)]
        pltpu.make_async_copy(part, part, recv1.at[t]).wait()
    for g in range(room):
        held[r, g] = landed[sources[g]]
    for s in range(1, nrow):
        spread(s).start()
    total[...] = jnp.zeros_like(total)
    load.wait()

    def give(d):
        return pltpu.make_async_remote_copy(
            src_ref=total.at[d], dst_ref=came.at[d], send_sem=send3.at[d], recv_sem=recv3.at[d],
            device_id=(r, lax.rem(c - d + ncol, ncol)), device_id_type=MESH)

    for s in range(1, nrow):
        arrived(s).wait_recv()

    def term(g, carry):
        pieces = [
            held[pl.ds(part * strips, strips), g].reshape(strips * STRIP, width) for part in range(parts)
        ]
        block = pieces[0] if parts == 1 else jnp.concatenate(pieces, axis=1)
        a_high, a_low = split(block)
        b_high, b_low = split(right_v[tab_idx[g]])
        value = dot(a_high, b_high) + (dot(a_high, b_low) + dot(a_low, b_high))
        for d in range(shifts):
            total[d] += tab_mask[d * room + g] * value
        return carry

    lax.fori_loop(0, room, term, 0)
    for d in range(1, shifts):
        give(d).start()

    result = total[0]
    for d in range(1, shifts):
        give(d).wait_recv()
        result = result + came[d]
    out[...] = result
    for d in range(1, shifts):
        give(d).wait_send()
    for d in range(shifts):
        @pl.when(my_d == d)
        def _():
            for s in range(1 if d == 0 else 0, nrow):
                scatter(d, s).wait_send()
    for s in range(1, nrow):
        spread(s).wait_send()


def body(left_rows, right_cols, left_pattern, right_pattern):
    nrow = lax.axis_size("row")
    ncol = lax.axis_size("col")
    ratio = nrow // ncol
    lrows, left_width = left_rows.shape
    right_height, blk = right_cols.shape
    per_k = left_width // blk
    trows = right_height // blk
    cap = per_k // 4
    shifts = STEPS // ratio
    strips = lrows // STRIP
    sizes = [size for size in SIZES if size[0] <= cap and size[1] < STEPS * cap] + [(cap, STEPS * cap)]
    smem = pl.BlockSpec(memory_space=pltpu.SMEM)
    vmem = pl.BlockSpec(memory_space=pltpu.VMEM)
    anywhere = pl.BlockSpec(memory_space=pl.ANY)
    across = right_pattern.T
    need, pick = pl.pallas_call(
        functools.partial(choose, (nrow, ncol, ratio, per_k, cap, blk), sizes),
        out_shape=(
            jax.ShapeDtypeStruct(left_pattern.shape, jnp.int32),
            jax.ShapeDtypeStruct((1,), jnp.int32),
        ),
        in_specs=[vmem, vmem],
        out_specs=(vmem, smem),
        name="choose",
    )(left_pattern, across)
    parts = nrow // strips
    dma = pltpu.SemaphoreType.DMA

    def run(number, slots, room):
        return pl.pallas_call(
            functools.partial(exchange, (nrow, ncol, ratio, per_k, slots, room, blk)),
            out_shape=jax.ShapeDtypeStruct((lrows, blk), jnp.float32),
            in_specs=[smem, smem, anywhere, anywhere],
            out_specs=vmem,
            scratch_shapes=[
                pltpu.VMEM((per_k, lrows, blk), jnp.float32),
                pltpu.VMEM((nrow, slots, STRIP, blk // parts), jnp.float32),
                pltpu.VMEM((STEPS * slots, STRIP, blk // parts), jnp.float32),
                pltpu.VMEM((nrow, room, STRIP, blk // parts), jnp.float32),
                pltpu.VMEM((trows, blk, blk), jnp.float32),
                pltpu.VMEM((shifts, lrows, blk), jnp.float32),
                pltpu.VMEM((shifts, lrows, blk), jnp.float32),
                pltpu.SMEM((room,), jnp.int32),
                pltpu.SMEM((shifts * room,), jnp.float32),
                dma, dma, dma((nrow,)), dma((STEPS,)), dma((nrow,)), dma((nrow,)), dma((shifts,)),
                dma((shifts,)),
            ],
            compiler_params=pltpu.CompilerParams(
                collective_id=number, has_side_effects=True, vmem_limit_bytes=60 * 1024 * 1024),
            name="exchange%d_%d" % (slots, room),
        )

    branches = [run(number, *size) for number, size in enumerate(sizes)]
    inputs = (need, across, left_rows, right_cols.reshape(trows, blk, blk))
    if len(branches) == 1:
        return branches[0](*inputs)
    return lax.switch(pick[0], branches, *inputs)


def solution(mesh):
    return jax.shard_map(
        body,
        mesh=mesh,
        in_specs=(P("col", "row"), P("col", "row"), P(), P()),
        out_specs=P("col", "row"),
        check_vma=False,
    )
```

```python
import functools

import jax
import jax.numpy as jnp
from jax import lax
from jax.experimental import pallas as pl
from jax.experimental.pallas import tpu as pltpu
from jax.sharding import PartitionSpec as P

STEPS = 4
STRIP = 8
SIZES = ((1, 4), (2, 5), (3, 6), (4, 6), (3, 9), (4, 9), (6, 12))
MESH = pl.DeviceIdType.MESH


def choose(dims, sizes, lpat, rpat, own, table, pick, need):
    nrow, ncol, ratio, per_k, cap, blk = dims
    shifts = STEPS // ratio
    useful = (lpat[...] != 0) & (jnp.max(rpat[...], axis=0, keepdims=True) != 0)
    useful = useful.astype(jnp.int32)
    need[...] = useful
    at = lax.broadcasted_iota(jnp.int32, useful.shape, 1)
    b = lax.broadcasted_iota(jnp.int32, (ncol, 1), 0)
    most = jnp.zeros((ncol, 1), jnp.int32)
    largest = jnp.zeros((1, 1), jnp.int32)
    for q in range(nrow):
        inside = (at >= q * per_k) & (at < (q + 1) * per_k)
        count = jnp.sum(jnp.where(inside, useful, 0), axis=1, keepdims=True)
        d = lax.rem(q // ratio - b + ncol, ncol)
        count = jnp.where(d < shifts, count, 0)
        most = jnp.maximum(most, count)
        group = count if q % ratio == 0 else group + count
        if q % ratio == ratio - 1:
            largest = jnp.maximum(largest, jnp.sum(group, axis=0, keepdims=True))
    top = jnp.max(most)
    full = jnp.max(largest)
    index = jnp.int32(len(sizes) - 1)
    for k in reversed(range(len(sizes) - 1)):
        index = jnp.where((top <= sizes[k][0]) & (full <= sizes[k][1]), k, index)
    pick[0] = index

    r = lax.axis_index("row")
    c = lax.axis_index("col")
    lanes = useful.shape[1]
    lane = lax.broadcasted_iota(jnp.int32, (1, lanes), 1)
    upper = lax.broadcasted_iota(jnp.int32, (lanes, lanes), 0) < lax.broadcasted_iota(jnp.int32, (lanes, lanes), 1)
    upper = upper.astype(jnp.float32).astype(jnp.bfloat16)
    slot = lax.broadcasted_iota(jnp.int32, own.shape, 0)
    entry = lax.broadcasted_iota(jnp.int32, table.shape, 0)

    def ranked(row, first):
        found = jnp.where((lane >= first) & (lane < first + per_k), need[pl.ds(row, 1), :], 0)
        return found, dot(found.astype(jnp.float32).astype(jnp.bfloat16), upper).astype(jnp.int32)

    found, rank = ranked(c, r * per_k)
    own[...] = jnp.sum(jnp.where((rank == slot) & (found != 0), lane - r * per_k, 0), axis=1, keepdims=True)
    held_by = (rpat[pl.ds(r, 1), :] != 0).astype(jnp.int32)
    codes = jnp.zeros(table.shape, jnp.int32)
    before = jnp.zeros((1, 1), jnp.int32)
    for t in range(STEPS):
        d, j = divmod(t, ratio)
        first = (c * ratio + j) * per_k
        found, rank = ranked(lax.rem(c - d + ncol, ncol), first)
        code = ((held_by * STEPS + t) * per_k + lane - first) * (cap + 1) + rank
        codes = codes + jnp.sum(jnp.where((rank + before == entry) & (found != 0), code, 0), axis=1, keepdims=True)
        before = before + jnp.sum(found, axis=1, keepdims=True)
    table[...] = codes


def split(x):
    high = x.astype(jnp.bfloat16)
    low = (x - high.astype(jnp.float32)).astype(jnp.bfloat16)
    return high, low


def dot(a, b):
    return jnp.dot(a, b, preferred_element_type=jnp.float32)


def exchange(dims, own, table, left, right, out, left_v, packed, landed, held, right_v, total, came, tab_idx,
             tab_mask, left_sem, right_sem, send1, recv1, send2, recv2, send3, recv3):
    nrow, ncol, ratio, per_k, most, cap, room, blk = dims
    shifts = STEPS // ratio
    strips = left.shape[0] // STRIP
    parts = nrow // strips
    width = blk // parts
    r = lax.axis_index("row")
    c = lax.axis_index("col")
    goal = r // ratio
    my_d = lax.rem(goal - c + ncol, ncol)
    my_j = lax.rem(r, ratio)

    @pl.when(my_d < shifts)
    def _():
        for u in range(per_k):
            pltpu.make_async_copy(left.at[:, pl.ds(u * blk, blk)], left_v.at[u], left_sem).start()

    load = pltpu.make_async_copy(right, right_v, right_sem)

    barrier = pltpu.get_barrier_semaphore()
    for s in range(1, nrow):
        pl.semaphore_signal(barrier, inc=1, device_id=(lax.rem(r + s, nrow), c), device_id_type=MESH)
    for d in range(1, shifts):
        behind = lax.rem(c - d + ncol, ncol)
        ahead = lax.rem(c + d, ncol)
        for j in range(ratio):
            pl.semaphore_signal(barrier, inc=1, device_id=(c * ratio + j, behind), device_id_type=MESH)
        pl.semaphore_signal(barrier, inc=1, device_id=(r, ahead), device_id_type=MESH)

    @pl.when(my_d < shifts)
    def _():
        pltpu.make_async_copy(left_v, left_v, left_sem).wait()
        for i in range(cap):
            block = left_v[own[i, 0]]
            for p in range(nrow):
                row, part = p % strips, p // strips
                packed[p, i] = block[row * STRIP:(row + 1) * STRIP, part * width:(part + 1) * width]

    base = nrow - 1 + shifts - 1
    sends = jnp.logical_and(my_d >= 1, my_d < shifts)
    pl.semaphore_wait(barrier, jnp.where(sends, base + nrow, base))

    def scatter(d, s):
        t = d * ratio + my_j
        p = lax.rem(r + s, nrow)
        return pltpu.make_async_remote_copy(
            src_ref=packed.at[p], dst_ref=landed.at[pl.ds(t * cap, cap)], send_sem=send1.at[s], recv_sem=recv1.at[t],
            device_id=(p, lax.rem(c + d, ncol)), device_id_type=MESH)

    def keep():
        return pltpu.make_async_copy(packed.at[r], landed.at[pl.ds(my_j * cap, cap)], recv1.at[my_j])

    for d in range(shifts):
        @pl.when(my_d == d)
        def _():
            if d == 0:
                keep().start()
            for s in range(1 if d == 0 else 0, nrow):
                scatter(d, s).start()

    def spread(s):
        return pltpu.make_async_remote_copy(
            src_ref=held.at[r], dst_ref=held.at[r], send_sem=send2.at[s], recv_sem=recv2.at[s],
            device_id=(lax.rem(r + s, nrow), c), device_id_type=MESH)

    def arrived(s):
        p = lax.rem(r - s + nrow, nrow)
        return pltpu.make_async_remote_copy(
            src_ref=held.at[p], dst_ref=held.at[p], send_sem=send2.at[s], recv_sem=recv2.at[s],
            device_id=(p, c), device_id_type=MESH)

    load.start()
    sources = []
    for g in range(room):
        code = table[g, 0]
        place = lax.rem(code, most + 1)
        code = lax.div(code, most + 1)
        inner = lax.rem(code, per_k)
        code = lax.div(code, per_k)
        t = lax.rem(code, STEPS)
        both = lax.div(code, STEPS)
        tab_idx[g] = lax.rem(t, ratio) * per_k + inner
        for d in range(shifts):
            tab_mask[d * room + g] = ((lax.div(t, ratio) == d).astype(jnp.int32) * both).astype(jnp.float32)
        sources.append(t * cap + place)
    for t in range(STEPS):
        part = landed.at[pl.ds(t * cap, cap)]
        pltpu.make_async_copy(part, part, recv1.at[t]).wait()
    for g in range(room):
        held[r, g] = landed[sources[g]]
    for s in range(1, nrow):
        spread(s).start()
    total[...] = jnp.zeros_like(total)
    load.wait()

    def give(d):
        return pltpu.make_async_remote_copy(
            src_ref=total.at[d], dst_ref=came.at[d], send_sem=send3.at[d], recv_sem=recv3.at[d],
            device_id=(r, lax.rem(c - d + ncol, ncol)), device_id_type=MESH)

    for s in range(1, nrow):
        arrived(s).wait_recv()

    def term(g, carry):
        pieces = [
            held[pl.ds(part * strips, strips), g].reshape(strips * STRIP, width) for part in range(parts)
        ]
        block = pieces[0] if parts == 1 else jnp.concatenate(pieces, axis=1)
        a_high, a_low = split(block)
        b_high, b_low = split(right_v[tab_idx[g]])
        value = dot(a_high, b_high) + (dot(a_high, b_low) + dot(a_low, b_high))
        for d in range(shifts):
            total[d] += tab_mask[d * room + g] * value
        return carry

    lax.fori_loop(0, room, term, 0)
    for d in range(1, shifts):
        give(d).start()

    result = total[0]
    for d in range(1, shifts):
        give(d).wait_recv()
        result = result + came[d]
    out[...] = result
    for d in range(1, shifts):
        give(d).wait_send()
    for d in range(shifts):
        @pl.when(my_d == d)
        def _():
            for s in range(1 if d == 0 else 0, nrow):
                scatter(d, s).wait_send()
    for s in range(1, nrow):
        spread(s).wait_send()


def body(left_rows, right_cols, left_pattern, right_pattern):
    nrow = lax.axis_size("row")
    ncol = lax.axis_size("col")
    ratio = nrow // ncol
    lrows, left_width = left_rows.shape
    right_height, blk = right_cols.shape
    per_k = left_width // blk
    trows = right_height // blk
    cap = per_k // 4
    shifts = STEPS // ratio
    strips = lrows // STRIP
    sizes = [size for size in SIZES if size[0] <= cap and size[1] < STEPS * cap] + [(cap, STEPS * cap)]
    smem = pl.BlockSpec(memory_space=pltpu.SMEM)
    vmem = pl.BlockSpec(memory_space=pltpu.VMEM)
    anywhere = pl.BlockSpec(memory_space=pl.ANY)
    across = right_pattern.T
    own, table, pick = pl.pallas_call(
        functools.partial(choose, (nrow, ncol, ratio, per_k, cap, blk), sizes),
        out_shape=(
            jax.ShapeDtypeStruct((STRIP, 1), jnp.int32),
            jax.ShapeDtypeStruct((STEPS * STRIP, 1), jnp.int32),
            jax.ShapeDtypeStruct((1,), jnp.int32),
        ),
        in_specs=[vmem, vmem],
        out_specs=(vmem, vmem, smem),
        scratch_shapes=[pltpu.VMEM(left_pattern.shape, jnp.int32)],
        name="choose",
    )(left_pattern, across)
    parts = nrow // strips
    dma = pltpu.SemaphoreType.DMA

    def run(number, slots, room):
        return pl.pallas_call(
            functools.partial(exchange, (nrow, ncol, ratio, per_k, cap, slots, room, blk)),
            out_shape=jax.ShapeDtypeStruct((lrows, blk), jnp.float32),
            in_specs=[smem, smem, anywhere, anywhere],
            out_specs=vmem,
            scratch_shapes=[
                pltpu.VMEM((per_k, lrows, blk), jnp.float32),
                pltpu.VMEM((nrow, slots, STRIP, blk // parts), jnp.float32),
                pltpu.VMEM((STEPS * slots, STRIP, blk // parts), jnp.float32),
                pltpu.VMEM((nrow, room, STRIP, blk // parts), jnp.float32),
                pltpu.VMEM((trows, blk, blk), jnp.float32),
                pltpu.VMEM((shifts, lrows, blk), jnp.float32),
                pltpu.VMEM((shifts, lrows, blk), jnp.float32),
                pltpu.SMEM((room,), jnp.int32),
                pltpu.SMEM((shifts * room,), jnp.float32),
                dma, dma, dma((nrow,)), dma((STEPS,)), dma((nrow,)), dma((nrow,)), dma((shifts,)),
                dma((shifts,)),
            ],
            compiler_params=pltpu.CompilerParams(
                collective_id=number, has_side_effects=True, vmem_limit_bytes=60 * 1024 * 1024),
            name="exchange%d_%d" % (slots, room),
        )

    branches = [run(number, *size) for number, size in enumerate(sizes)]
    inputs = (own, table, left_rows, right_cols.reshape(trows, blk, blk))
    if len(branches) == 1:
        return branches[0](*inputs)
    return lax.switch(pick[0], branches, *inputs)


def solution(mesh):
    return jax.shard_map(
        body,
        mesh=mesh,
        in_specs=(P("col", "row"), P("col", "row"), P(), P()),
        out_specs=P("col", "row"),
        check_vma=False,
    )
```
